32 devices in a mesh: dp: 8 (over z, x), tensor: 4 (over y, core).
Axes of the slice: x: 2, y: 2, z: 4, core: 2. Of those that a mesh axis runs over, the one named last changes fastest.
Arguments:
- tokens: bfloat16 [1024, 4096], P('dp', 'tensor'), may hold values from -6 to 6
- out_grad: bfloat16 [1024, 4096], P('dp', 'tensor'), may hold values from -6 to 6
- up_weight: bfloat16 [4096, 3584], P('dp', 'tensor'), may hold values from -0.09375 to 0.09375
- down_weight: bfloat16 [3584, 4096], P('tensor', 'dp'), may hold values from -0.09375 to 0.09375
- up_accum: float32 [8, 256, 3584], P('dp', None, 'tensor'), may hold values from -6 to 6
- down_accum: float32 [8, 3584, 256], P('dp', 'tensor'), may hold values from -6 to 6
- up_q: float32 [3584, 32], P('tensor'), may hold values from -6 to 6
- down_q: float32 [256, 32], replicated, may hold values from -6 to 6
Outputs:
- input_grad: bfloat16 [1024, 4096], P('dp', 'tensor')
- up_error: float32 [8, 256, 3584], P('dp', None, 'tensor')
- up_left: float32 [256, 32], replicated
- up_right: float32 [3584, 32], P('tensor')
- down_error: float32 [8, 3584, 256], P('dp', 'tensor')
- down_left: float32 [3584, 32], P('tensor')
- down_right: float32 [256, 32], replicated
The draws below stay inside these ranges and needn't reach their ends.
All inputs are finite; a program needn't handle non-finite values.
Results may differ from the reference program's by a relative error of at most 0.02.
Values may be sent and summed in bfloat16 or wider, within the bound.
No kernel may reach another device: no remote copies, remote signals or barrier semaphores. Data moves between devices by JAX's collectives and lax.ppermute only.
A program may use at most 128 MiB of HBM per device.

```python
import math
import jax
import jax.numpy as jnp
from jax import lax

D = 4096
FF_DEV = 896
TOK = 128
WIN = 256
RANK = 32
FF = 3584
TOKENS = 1024
N_DP = 8
N_TENSOR = 4


def shard_levels(rng, shape, shards, low, top_value):
    factor_of = 1.0
    for position, blocks in shards:
        heights = jax.random.uniform(jax.random.fold_in(jax.random.fold_in(rng, 6), position), (blocks,), jnp.float32, low / len(shards), top_value / len(shards))
        factor_of = factor_of * jnp.repeat(jnp.exp(heights), shape[position] // blocks).reshape((-1,) + (1,) * (len(shape) - 1 - position))
    return factor_of


def gaussian(rng, dims, deviation, limit, pieces=(), held_as=jnp.bfloat16):
    loudness = shard_levels(rng, dims, pieces, -0.22, 0.18) if pieces else 1.0
    result = jax.random.normal(rng, dims, jnp.float32) * deviation * loudness
    return jnp.minimum(jnp.maximum(result, -limit), limit).astype(held_as)


def setup_inputs(seed: int = 0) -> dict:
    arg_keys = jax.random.split(jax.random.key(seed), 9)
    tokens = gaussian(arg_keys[0], (TOKENS, D), 1.0, 6.0, ((0, 8), (1, 4)))
    out_grad = gaussian(arg_keys[1], (TOKENS, D), 1.0, 6.0, ((0, 8), (1, 4)))
    up_weight = gaussian(arg_keys[2], (D, FF), D ** -0.5, 0.09375, ((0, 8), (1, 4)))
    down_weight = gaussian(arg_keys[3], (FF, D), FF ** -0.5, 0.09375, ((0, 4), (1, 8)))
    up_accum = gaussian(arg_keys[4], (N_DP, WIN, FF), 1.0, 6.0, ((0, 8), (2, 4)), jnp.float32)
    down_accum = gaussian(arg_keys[5], (N_DP, FF, WIN), 1.0, 6.0, ((0, 8), (1, 4)), jnp.float32)
    up_q = gaussian(arg_keys[6], (FF, RANK), 1.0, 6.0, ((0, 4),), jnp.float32)
    down_q = gaussian(arg_keys[7], (WIN, RANK), 1.0, 6.0, (), jnp.float32)
    return dict(tokens=tokens, out_grad=out_grad, up_weight=up_weight, down_weight=down_weight, up_accum=up_accum, down_accum=down_accum, up_q=up_q, down_q=down_q)


def orthonormal(left_sum):
    gram = jnp.dot(left_sum.T, left_sum, precision=lax.Precision.HIGHEST)
    lower_factor = jnp.linalg.cholesky(gram)
    return lax.linalg.triangular_solve(lower_factor, left_sum, left_side=False, lower=True, transpose_a=True)

def compress(matrix, start_q):
    left_sum = jnp.einsum('rab,bk->ak', matrix, start_q, precision=lax.Precision.HIGHEST)
    left = orthonormal(left_sum)
    right = jnp.einsum('rab,ak->bk', matrix, left, precision=lax.Precision.HIGHEST) / N_DP
    approx = jnp.dot(left, right.T, precision=lax.Precision.HIGHEST)
    return (matrix - approx[None], left, right)

def reference(tokens, out_grad, up_weight, down_weight, up_accum, down_accum, up_q, down_q):
    preact = jnp.dot(tokens.astype(jnp.float32), up_weight.astype(jnp.float32), preferred_element_type=jnp.float32)
    back_act = jnp.dot(out_grad.astype(jnp.float32), down_weight.T.astype(jnp.float32), preferred_element_type=jnp.float32)
    squash = jax.nn.sigmoid(preact)
    act_out = (preact * squash).astype(jnp.bfloat16)
    hidden_grad = (back_act * squash * (1.0 + preact * (1.0 - squash))).astype(jnp.bfloat16)
    grad_blocks = hidden_grad.reshape(TOKENS, N_TENSOR, FF_DEV).transpose(1, 0, 2)
    weight_blocks = up_weight.reshape(D, N_TENSOR, FF_DEV).transpose(1, 0, 2)

    def add_block(running, blocks):
        partial_sum = jnp.dot(blocks[0].astype(jnp.float32), blocks[1].T.astype(jnp.float32), preferred_element_type=jnp.float32)
        rounded = lax.optimization_barrier(partial_sum.astype(jnp.bfloat16))
        return (running + rounded.astype(jnp.float32), 0)
    running, unused = lax.scan(add_block, jnp.zeros((TOKENS, D), jnp.float32), (grad_blocks, weight_blocks))
    input_grad = running.astype(jnp.bfloat16)
    grad_scale = 1.0 / math.sqrt(TOK)
    token_window = tokens.reshape(N_DP, TOK, D)[:, :, :WIN].astype(jnp.float32)
    grad_window = out_grad.reshape(N_DP, TOK, D)[:, :, :WIN].astype(jnp.float32)
    hidden_rep = hidden_grad.reshape(N_DP, TOK, FF).astype(jnp.float32)
    act_rep = act_out.reshape(N_DP, TOK, FF).astype(jnp.float32)
    up_matrix = up_accum + jnp.einsum('rtw,rtf->rwf', token_window, hidden_rep, precision=lax.Precision.HIGHEST) * grad_scale
    down_matrix = down_accum + jnp.einsum('rtf,rtw->rfw', act_rep, grad_window, precision=lax.Precision.HIGHEST) * grad_scale
    up_error, up_left, up_right = compress(up_matrix, up_q)
    down_error, down_left, down_right = compress(down_matrix, down_q)
    return (input_grad, up_error, up_left, up_right, down_error, down_left, down_right)
```

```python
import math

import jax
import jax.numpy as jnp
from jax import lax
from jax.sharding import PartitionSpec as P

BF = jnp.bfloat16
F32 = jnp.float32
HIGHEST = lax.Precision.HIGHEST


def flip(arr, axis, mask):
    size = lax.axis_size(axis)
    return lax.ppermute(arr, axis, [(i, i ^ mask) for i in range(size)])


def bits_of(size):
    return [1 << b for b in range(size.bit_length() - 1)]


def dot(a, b, dims=((1,), (0,)), precision=None):
    return lax.dot_general(a, b, (dims, ((), ())), preferred_element_type=F32, precision=precision)


def allsum(arr, axis, masks):
    for mask in masks:
        arr = arr + flip(arr, axis, mask)
    return arr


def broadcast_first(arr, axis):
    arr = jnp.where(lax.axis_index(axis) == 0, arr, jnp.zeros_like(arr))
    for mask in bits_of(lax.axis_size(axis)):
        arr = arr + lax.ppermute(arr, axis, [(i, i + mask) for i in range(mask)])
    return arr


def inverse_factor(gram):
    lower = jnp.linalg.cholesky(gram)
    return lax.linalg.triangular_solve(
        lower, jnp.eye(gram.shape[0], dtype=F32), left_side=False, lower=True, transpose_a=True
    )


def spread(arr, half, core, zrel, zbits, tbits):
    rows, width = arr.shape
    lo, hi = arr[:, : width // 2], arr[:, width // 2 :]
    mine = jnp.where(half == 0, lo, hi)
    other = jnp.where(half == 0, hi, lo)
    blocks = jnp.stack([mine, flip(other, "tensor", 1)])
    for mask in tbits[1:]:
        blocks = jnp.concatenate([blocks, flip(blocks, "tensor", mask)])
    count = blocks.shape[0]
    kept = []
    for k in range(count):
        piece = lax.dynamic_index_in_dim(blocks, zrel ^ k, 0, keepdims=False)
        kept.append(piece if k == 0 else flip(piece, "dp", 2 * k))
    kept = jnp.stack(kept)
    return kept, flip(kept, "tensor", 1)


def reduce_z(part_of, zbits):
    count = 2 ** len(zbits)
    first = zbits[0]
    out_ks = [k for k in range(count) if k & first]
    keep_ks = [k for k in range(count) if not k & first]
    got = flip(part_of(out_ks).astype(BF), "dp", 2 * first)
    acc = part_of(keep_ks) + got.astype(F32)
    for bit in zbits[1:]:
        sel = [n for n, k in enumerate(keep_ks) if k & bit]
        stay = [n for n, k in enumerate(keep_ks) if not k & bit]
        send = jnp.stack([acc[n] for n in sel]).astype(BF)
        acc = jnp.stack([acc[n] for n in stay]) + flip(send, "dp", 2 * bit).astype(F32)
        keep_ks = [keep_ks[n] for n in stay]
    return acc[0]


def shards(tokens, out_grad, up_weight, down_weight, up_accum, down_accum, up_q, down_q):
    replicas, columns = lax.axis_size("dp"), lax.axis_size("tensor")
    dp_i, t_i = lax.axis_index("dp"), lax.axis_index("tensor")
    x_i, z_i = dp_i % 2, dp_i // 2
    core = t_i % 2
    zcount = replicas // 2
    zbits, tbits, dbits = bits_of(zcount), bits_of(columns), bits_of(replicas)
    rows, width = tokens.shape
    window = up_accum.shape[1]
    scale = 1.0 / math.sqrt(rows)
    half = core ^ x_i
    zrel = z_i ^ t_i

    up_other = flip(up_weight, "dp", 1)
    tok_keep, tok_other = spread(tokens, half, core, zrel, zbits, tbits)
    down_other = flip(down_weight, "dp", 1)
    grad_keep, grad_other = spread(out_grad, half, core, zrel, zbits, tbits)
    windows = broadcast_first(jnp.stack([tokens[:, :window], out_grad[:, :window]]), "tensor")
    tok_win, grad_win = windows[0], windows[1]

    def partial(kept, other, own_w, par_w, dims):
        lhs_own = jnp.where(core == 0, kept, other)
        lhs_par = jnp.where(core == 0, other, kept)

        def part_of(ks):
            a = jnp.concatenate([lhs_own[k] for k in ks])
            b = jnp.concatenate([lhs_par[k] for k in ks])
            return (dot(a, own_w, dims) + dot(b, par_w, dims)).reshape(len(ks), rows, -1)

        return part_of

    preact = reduce_z(partial(tok_keep, tok_other, up_weight, up_other, ((1,), (0,))), zbits)
    back_act = reduce_z(partial(grad_keep, grad_other, down_weight, down_other, ((1,), (1,))), zbits)
    squash = jax.nn.sigmoid(preact)
    act_out = (preact * squash).astype(BF)
    hidden = (back_act * squash * (1.0 + preact * (1.0 - squash))).astype(BF)

    down_matrix = down_accum[0] + dot(act_out, grad_win, ((0,), (0,))) * scale
    down_sum = allsum(dot(down_matrix, down_q, precision=HIGHEST), "dp", dbits)
    down_gram = dot(down_sum, down_sum, ((0,), (0,)), HIGHEST)
    down_term = dot(down_matrix, down_sum, ((0,), (0,)), HIGHEST)
    both = allsum(jnp.concatenate([down_term, down_gram]), "tensor", tbits)
    down_gram = both[window:]
    down_term = allsum(both[:window], "dp", dbits)
    down_inv = inverse_factor(down_gram)
    down_left = dot(down_sum, down_inv, precision=HIGHEST)
    down_right = dot(down_term, down_inv, precision=HIGHEST) / replicas
    down_error = down_matrix - dot(down_left, down_right, ((1,), (1,)), HIGHEST)

    gathered = {0: hidden}
    for bit in reversed(zbits):
        ks = sorted(gathered)
        got = flip(jnp.stack([gathered[k] for k in ks]), "dp", 2 * bit)
        for n, k in enumerate(ks):
            gathered[k | bit] = got[n]
    up_matrix = up_accum[0] + dot(tok_win, hidden, ((0,), (0,))) * scale
    up_sum = allsum(allsum(dot(up_matrix, up_q, precision=HIGHEST), "tensor", tbits), "dp", dbits)
    up_term = allsum(dot(up_matrix, up_sum, ((0,), (0,)), HIGHEST), "dp", dbits)
    up_inv = inverse_factor(dot(up_sum, up_sum, ((0,), (0,)), HIGHEST))
    up_left = dot(up_sum, up_inv, precision=HIGHEST)
    up_right = dot(up_term, up_inv, precision=HIGHEST) / replicas
    up_error = up_matrix - dot(up_left, up_right, ((1,), (1,)), HIGHEST)

    hid = jnp.concatenate([gathered[k] for k in range(zcount)])
    w_keep = jnp.where(core == 0, up_weight, up_other)
    w_send = jnp.where(core == 0, up_other, up_weight)
    send = dot(hid, w_send, ((1,), (1,))).astype(BF)
    keep = dot(hid, w_keep, ((1,), (1,))).astype(BF)
    mine = (keep.astype(F32) + flip(send, "tensor", 1).astype(F32)).astype(BF)
    mine = mine.reshape(zcount, 1, rows, width // 2)
    for bit in zbits:
        mine = mine.reshape((mine.shape[0] // 2, 2) + mine.shape[1:])
        got = flip(mine[:, 1], "dp", 2 * bit)
        mine = jnp.concatenate([mine[:, 0], got], axis=1)
    blocks = mine[0]
    blocks = jnp.stack(
        [lax.dynamic_index_in_dim(blocks, zrel ^ j, 0, keepdims=False) for j in range(columns)]
    )
    for mask in reversed(tbits[1:]):
        n = blocks.shape[0] // 2
        got = flip(blocks[n:], "tensor", mask)
        blocks = (blocks[:n].astype(F32) + got.astype(F32)).astype(BF)
    got = flip(blocks[1], "tensor", 1)
    input_grad = jnp.concatenate(
        [jnp.where(half == 0, blocks[0], got), jnp.where(half == 0, got, blocks[0])], axis=1
    )
    return (input_grad, up_error[None], up_left, up_right, down_error[None], down_left, down_right)


def solution(mesh):
    return jax.shard_map(
        shards,
        mesh=mesh,
        in_specs=(
            P("dp", "tensor"),
            P("dp", "tensor"),
            P("dp", "tensor"),
            P("tensor", "dp"),
            P("dp", None, "tensor"),
            P("dp", "tensor", None),
            P("tensor", None),
            P(),
        ),
        out_specs=(
            P("dp", "tensor"),
            P("dp", None, "tensor"),
            P(),
            P("tensor", None),
            P("dp", "tensor", None),
            P("tensor", None),
            P(),
        ),
        check_vma=False,
    )
```

```python
import math

import jax
import jax.numpy as jnp
from jax import lax
from jax.sharding import PartitionSpec as P

BF = jnp.bfloat16
F32 = jnp.float32
HIGHEST = lax.Precision.HIGHEST


def flip(arr, axis, mask):
    size = lax.axis_size(axis)
    return lax.ppermute(arr, axis, [(i, i ^ mask) for i in range(size)])


def bits_of(size):
    return [1 << b for b in range(size.bit_length() - 1)]


def dot(a, b, dims=((1,), (0,)), precision=None):
    return lax.dot_general(a, b, (dims, ((), ())), preferred_element_type=F32, precision=precision)


def allsum(arr, axis, masks):
    for mask in masks:
        arr = arr + flip(arr, axis, mask)
    return arr


def broadcast_first(arr, axis):
    arr = jnp.where(lax.axis_index(axis) == 0, arr, jnp.zeros_like(arr))
    for mask in bits_of(lax.axis_size(axis)):
        arr = arr + lax.ppermute(arr, axis, [(i, i + mask) for i in range(mask)])
    return arr


def inverse_factor(gram):
    lower = jnp.linalg.cholesky(gram)
    return lax.linalg.triangular_solve(
        lower, jnp.eye(gram.shape[0], dtype=F32), left_side=False, lower=True, transpose_a=True
    )


def tie(*arrs):
    return lax.optimization_barrier(arrs)


def first_half(count):
    return (count // 2 + 127) // 128 * 128


def exchange_tensor(arr, half, tbits):
    width = arr.shape[1] // 2
    lo, hi = arr[:, :width], arr[:, width:]
    mine = jnp.where(half == 0, lo, hi)
    other = jnp.where(half == 0, hi, lo)
    blocks = [mine, flip(other, "tensor", 1)]
    for mask in tbits[1:]:
        got = flip(jnp.stack(blocks), "tensor", mask)
        blocks = blocks + [got[n] for n in range(len(blocks))]
    return jnp.stack(blocks)


def exchange_z(blocks, zrel):
    kept = []
    for k in range(blocks.shape[0]):
        piece = lax.dynamic_index_in_dim(blocks, zrel ^ k, 0, keepdims=False)
        kept.append(piece if k == 0 else flip(piece, "dp", 2 * k))
    return kept


def shards(tokens, out_grad, up_weight, down_weight, up_accum, down_accum, up_q, down_q):
    replicas, columns = lax.axis_size("dp"), lax.axis_size("tensor")
    dp_i, t_i = lax.axis_index("dp"), lax.axis_index("tensor")
    x_i, z_i = dp_i % 2, dp_i // 2
    core = t_i % 2
    zcount = replicas // 2
    zbits, tbits, dbits = bits_of(zcount), bits_of(columns), bits_of(replicas)
    rows, width = tokens.shape
    window = up_accum.shape[1]
    scale = 1.0 / math.sqrt(rows)
    half = core ^ x_i
    zrel = z_i ^ t_i

    ucut, dcut = first_half(up_weight.shape[0]), first_half(down_weight.shape[0])
    up_a = flip(up_weight[:ucut], "dp", 1)
    tok_blocks = exchange_tensor(tokens, half, tbits)
    grad_blocks = exchange_tensor(out_grad, half, tbits)
    tok_blocks, up_a = tie(tok_blocks, up_a)
    up_b_in, up_a = tie(up_weight[ucut:], up_a)
    up_b = flip(up_b_in, "dp", 1)
    tok_keep = exchange_z(tok_blocks, zrel)
    windows = broadcast_first(jnp.stack([tokens[:, :window], out_grad[:, :window]]), "tensor")
    grad_keep = exchange_z(grad_blocks, zrel)
    tok_keep[1], up_b = tie(tok_keep[1], up_b)
    tok_other = [flip(piece, "tensor", 1) for piece in tok_keep]
    down_a_in, up_b = tie(down_weight[:dcut], up_b)
    down_a = flip(down_a_in, "dp", 1)
    grad_other = [flip(piece, "tensor", 1) for piece in grad_keep]
    up_other = jnp.concatenate([up_a, up_b])
    tok_win, grad_win = windows[0], windows[1]

    def partial(kept, other, own_w, par_w, dims):
        def part_of(ks):
            a = jnp.concatenate([jnp.where(core == 0, kept[k], other[k]) for k in ks])
            b = jnp.concatenate([jnp.where(core == 0, other[k], kept[k]) for k in ks])
            return (dot(a, own_w, dims) + dot(b, par_w, dims)).reshape(len(ks), rows, -1)

        return part_of

    def first_stage(part_of):
        send = [k for k in range(zcount) if k & 1]
        keep = [k for k in range(zcount) if not k & 1]
        got = flip(part_of(send).astype(BF), "dp", 2)
        return part_of(keep) + got.astype(F32)

    def later_stages(acc):
        ks = [k for k in range(zcount) if not k & 1]
        for bit in zbits[1:]:
            sel = [n for n, k in enumerate(ks) if k & bit]
            stay = [n for n, k in enumerate(ks) if not k & bit]
            send = jnp.stack([acc[n] for n in sel]).astype(BF)
            acc = jnp.stack([acc[n] for n in stay]) + flip(send, "dp", 2 * bit).astype(F32)
            ks = [ks[n] for n in stay]
        return acc[0]

    pre_acc = first_stage(partial(tok_keep, tok_other, up_weight, up_other, ((1,), (0,))))
    pre_acc, down_a = tie(pre_acc, down_a)
    down_b_in, down_a = tie(down_weight[dcut:], down_a)
    down_b = flip(down_b_in, "dp", 1)
    preact = later_stages(pre_acc)
    down_other = jnp.concatenate([down_a, down_b])
    back_acc = first_stage(partial(grad_keep, grad_other, down_weight, down_other, ((1,), (1,))))
    back_act = later_stages(back_acc)

    squash = jax.nn.sigmoid(preact)
    act_out = (preact * squash).astype(BF)
    slope = squash * (1.0 + preact * (1.0 - squash))
    down_matrix = down_accum[0] + dot(act_out, grad_win, ((0,), (0,))) * scale
    down_sum = allsum(dot(down_matrix, down_q, precision=HIGHEST), "dp", dbits)
    down_gram = dot(down_sum, down_sum, ((0,), (0,)), HIGHEST)
    down_term = dot(down_matrix, down_sum, ((0,), (0,)), HIGHEST)
    back_act, down_gram, down_term = tie(back_act, down_gram, down_term)
    hidden = (back_act * slope).astype(BF)

    w_dims = ((1,), (1,))
    hid = {0: hidden}
    returned = {}

    def send_back(ks):
        lhs = jnp.concatenate([hid[k] for k in ks])
        own = dot(lhs, up_weight, w_dims).astype(BF)
        par = dot(lhs, up_other, w_dims).astype(BF)
        got = flip(jnp.where(core == 0, par, own), "tensor", 1)
        mine = (jnp.where(core == 0, own, par).astype(F32) + got.astype(F32)).astype(BF)
        mine = mine.reshape(len(ks), rows, -1)
        for n, k in enumerate(ks):
            returned[k] = mine[n] if k == 0 else flip(mine[n], "dp", 2 * k)

    def settle(ks):
        blocks = [returned[k] for k in ks]
        stack = jnp.stack(blocks)
        order = [
            lax.dynamic_index_in_dim(stack, (zrel >> 1) ^ q, 0, keepdims=False) for q in range(len(ks))
        ]
        for mask in reversed(tbits[1:]):
            n = len(order) // 2
            got = flip(jnp.stack(order[n:]), "tensor", mask)
            order = [(order[i].astype(F32) + got[i].astype(F32)).astype(BF) for i in range(n)]
        return order[0]

    for bit in reversed(zbits[1:]):
        ks = sorted(hid)
        got = flip(jnp.stack([hid[k] for k in ks]), "dp", 2 * bit)
        for n, k in enumerate(ks):
            hid[k | bit] = got[n]
    even = sorted(hid)
    got = flip(jnp.stack([hid[k] for k in even]), "dp", 2)
    send_back(even)
    for n, k in enumerate(even):
        hid[k | 1] = got[n]
    send_back([k | 1 for k in even])
    sum_a = settle(even)
    sum_b = settle([k | 1 for k in even])
    low = zrel & 1
    got = flip(jnp.where(low == 0, sum_b, sum_a), "tensor", 1)
    own = jnp.where(low == 0, sum_a, sum_b)
    input_grad = jnp.concatenate(
        [jnp.where(half == 0, own, got), jnp.where(half == 0, got, own)], axis=1
    )

    up_matrix = up_accum[0] + dot(tok_win, hidden, ((0,), (0,))) * scale
    both = jnp.concatenate([dot(up_matrix, up_q, precision=HIGHEST), down_term, down_gram])
    both = allsum(allsum(both, "tensor", tbits), "dp", dbits)
    up_sum, down_term, down_gram = both[:window], both[window : 2 * window], both[2 * window :]
    up_term = allsum(dot(up_matrix, up_sum, ((0,), (0,)), HIGHEST), "dp", dbits)
    up_inv = inverse_factor(dot(up_sum, up_sum, ((0,), (0,)), HIGHEST))
    up_left = dot(up_sum, up_inv, precision=HIGHEST)
    up_right = dot(up_term, up_inv, precision=HIGHEST) / replicas
    up_error = up_matrix - dot(up_left, up_right, ((1,), (1,)), HIGHEST)
    down_inv = inverse_factor(down_gram / replicas)
    down_left = dot(down_sum, down_inv, precision=HIGHEST)
    down_right = dot(down_term, down_inv, precision=HIGHEST) / replicas
    down_error = down_matrix - dot(down_left, down_right, ((1,), (1,)), HIGHEST)
    return (input_grad, up_error[None], up_left, up_right, down_error[None], down_left, down_right)


def solution(mesh):
    return jax.shard_map(
        shards,
        mesh=mesh,
        in_specs=(
            P("dp", "tensor"),
            P("dp", "tensor"),
            P("dp", "tensor"),
            P("tensor", "dp"),
            P("dp", None, "tensor"),
            P("dp", "tensor", None),
            P("tensor", None),
            P(),
        ),
        out_specs=(
            P("dp", "tensor"),
            P("dp", None, "tensor"),
            P(),
            P("tensor", None),
            P("dp", "tensor", None),
            P("tensor", None),
            P(),
        ),
        check_vma=False,
    )
```

```python
import math

import jax
import jax.numpy as jnp
from jax import lax
from jax.experimental import pallas as pl
from jax.experimental.pallas import tpu as pltpu
from jax.sharding import PartitionSpec as P

BF = jnp.bfloat16
F32 = jnp.float32
HIGHEST = lax.Precision.HIGHEST


def flip(arr, axis, mask):
    size = lax.axis_size(axis)
    return lax.ppermute(arr, axis, [(i, i ^ mask) for i in range(size)])


def bits_of(size):
    return [1 << b for b in range(size.bit_length() - 1)]


def dot(a, b, dims=((1,), (0,)), precision=None):
    return lax.dot_general(a, b, (dims, ((), ())), preferred_element_type=F32, precision=precision)


def factor_kernel(up_ref, down_ref, up_out, down_out):
    rank = up_ref.shape[0]
    row_id = lax.broadcasted_iota(jnp.int32, (rank, 2 * rank), 0)
    col_id = lax.broadcasted_iota(jnp.int32, (rank, 2 * rank), 1)
    eye = (row_id + rank == col_id).astype(F32)
    state = [
        eye + jnp.concatenate([ref[...], jnp.zeros((rank, rank), F32)], axis=1)
        for ref in (up_ref, down_ref)
    ]
    for j in range(rank):
        for n in range(2):
            aug = state[n]
            root = lax.rsqrt(aug[j : j + 1, j : j + 1])
            row = aug[j : j + 1, :] * root
            col = aug[:, j : j + 1] * root
            state[n] = jnp.where(row_id > j, aug - col * row, jnp.where(row_id == j, row, aug))
    up_out[...] = state[0][:, rank:]
    down_out[...] = state[1][:, rank:]


def inverse_factors(up_gram, down_gram):
    shape = jax.ShapeDtypeStruct(up_gram.shape, F32)
    return pl.pallas_call(
        factor_kernel,
        out_shape=(shape, shape),
        name="inverse_factors",
        cost_estimate=pl.CostEstimate(flops=10**6, bytes_accessed=20000, transcendentals=64),
    )(up_gram, down_gram)


class Order:
    def __init__(self):
        self.last = None

    def __call__(self, arr):
        if self.last is not None:
            arr, self.last = lax.optimization_barrier((arr, self.last))
        self.last = arr
        return arr


def tie(*arrs):
    return lax.optimization_barrier(arrs)


def split_half(arr, half):
    width = arr.shape[1] // 2
    lo, hi = arr[:, :width], arr[:, width:]
    return jnp.where(half == 0, lo, hi), jnp.where(half == 0, hi, lo)


def shards(tokens, out_grad, up_weight, down_weight, up_accum, down_accum, up_q, down_q):
    replicas, columns = lax.axis_size("dp"), lax.axis_size("tensor")
    dp_i, t_i = lax.axis_index("dp"), lax.axis_index("tensor")
    x_i, z_i = dp_i % 2, dp_i // 2
    core = t_i % 2
    zcount = replicas // 2
    zbits, tbits, dbits = bits_of(zcount), bits_of(columns), bits_of(replicas)
    rows = tokens.shape[0]
    window = up_accum.shape[1]
    scale = 1.0 / math.sqrt(rows)
    half = core ^ x_i
    zrel = z_i ^ t_i
    wait = Order()

    def send_z(blocks):
        kept = []
        for k in range(blocks.shape[0]):
            piece = lax.dynamic_index_in_dim(blocks, zrel ^ k, 0, keepdims=False)
            kept.append(piece if k == 0 else flip(piece, "dp", 2 * k))
        return kept

    ucut = (up_weight.shape[0] * 3 // 8 + 63) // 64 * 64
    dcut = (down_weight.shape[0] // 2 + 127) // 128 * 128
    up_a = flip(up_weight[:ucut], "dp", 1)
    mine, swap = split_half(tokens, half)
    tok_blocks = [mine, wait(flip(swap, "tensor", 1))]
    got = flip(jnp.stack(tok_blocks), "tensor", tbits[1])
    grad_in, tok_win, grad_win, wait.last = tie(
        out_grad, tokens[:, :window], out_grad[:, :window], wait.last
    )
    mine, swap = split_half(grad_in, half)
    swap = flip(swap, "tensor", 1)
    windows = jnp.stack([tok_win, grad_win])
    windows = jnp.where(t_i == 0, windows, jnp.zeros_like(windows))
    win_got = lax.ppermute(windows, "tensor", [(0, 1)])
    grad_blocks = [mine, wait(swap)]
    for mask in tbits[1:]:
        if mask > tbits[1]:
            got = flip(jnp.stack(tok_blocks), "tensor", mask)
        got = wait(got)
        tok_blocks = tok_blocks + [got[n] for n in range(len(tok_blocks))]
    tok_keep = send_z(jnp.stack(tok_blocks))
    up_a = wait(up_a)
    up_b_in, up_a = tie(up_weight[ucut:], up_a)
    up_b = flip(up_b_in, "dp", 1)
    windows = windows + wait(win_got)
    grad_got = flip(jnp.stack(grad_blocks), "tensor", tbits[1])
    win_got = lax.ppermute(windows, "tensor", [(0, 2), (1, 3)])
    tok_keep = [tok_keep[0]] + [wait(piece) for piece in tok_keep[1:]]
    for mask in tbits[1:]:
        if mask > tbits[1]:
            grad_got = flip(jnp.stack(grad_blocks), "tensor", mask)
        grad_got = wait(grad_got)
        grad_blocks = grad_blocks + [grad_got[n] for n in range(len(grad_blocks))]
    grad_keep = send_z(jnp.stack(grad_blocks))
    windows = windows + wait(win_got)
    for mask in tbits[2:]:
        windows = windows + wait(
            lax.ppermute(windows, "tensor", [(i, i + mask) for i in range(mask)])
        )
    tok_win, grad_win = windows[0], windows[1]
    up_b = wait(up_b)
    down_a_in, up_b = tie(down_weight[:dcut], up_b)
    down_a = flip(down_a_in, "dp", 1)
    up_other = jnp.concatenate([up_a, up_b])

    def other_halves(kept):
        got = [flip(piece, "tensor", 1) for piece in kept]
        return [wait(piece) for piece in got]

    def partial(kept, other, own_w, par_w, dims):
        def part_of(ks):
            a = jnp.concatenate([jnp.where(core == 0, kept[k], other[k]) for k in ks])
            b = jnp.concatenate([jnp.where(core == 0, other[k], kept[k]) for k in ks])
            return (dot(a, own_w, dims) + dot(b, par_w, dims)).reshape(len(ks), rows, -1)

        return part_of

    odd = [k for k in range(zcount) if k & 1]
    even = [k for k in range(zcount) if not k & 1]

    def later_stages(acc):
        ks = even
        for bit in zbits[1:]:
            sel = [n for n, k in enumerate(ks) if k & bit]
            stay = [n for n, k in enumerate(ks) if not k & bit]
            send = jnp.stack([acc[n] for n in sel]).astype(BF)
            acc = jnp.stack([acc[n] for n in stay]) + wait(flip(send, "dp", 2 * bit)).astype(F32)
            ks = [ks[n] for n in stay]
        return acc[0]

    tok_other = other_halves(tok_keep)
    part_of = partial(tok_keep, tok_other, up_weight, up_other, ((1,), (0,)))
    pre_got = flip(part_of(odd).astype(BF), "dp", 2)
    pre_acc = part_of(even)
    down_a = wait(down_a)
    down_b_in, down_a = tie(down_weight[dcut:], down_a)
    down_b = flip(down_b_in, "dp", 1)
    grad_keep = [grad_keep[0]] + [wait(piece) for piece in grad_keep[1:]]
    pre_acc = pre_acc + wait(pre_got).astype(F32)
    grad_other = other_halves(grad_keep)
    down_b = wait(down_b)
    down_other = jnp.concatenate([down_a, down_b])
    part_of = partial(grad_keep, grad_other, down_weight, down_other, ((1,), (1,)))
    back_got = flip(part_of(odd).astype(BF), "dp", 2)
    back_acc = part_of(even)
    preact = later_stages(pre_acc)

    squash = jax.nn.sigmoid(preact)
    act_out = (preact * squash).astype(BF)
    slope = squash * (1.0 + preact * (1.0 - squash))
    down_matrix = down_accum[0] + dot(act_out, grad_win, ((0,), (0,))) * scale
    down_sum = dot(down_q, down_matrix, ((0,), (1,)), HIGHEST)
    down_sum = down_sum + wait(flip(down_sum, "dp", 1))
    back_acc = back_acc + wait(back_got).astype(F32)
    for mask in dbits[1:-1]:
        down_sum = down_sum + wait(flip(down_sum, "dp", mask))
    down_got = flip(down_sum, "dp", dbits[-1])
    back_act = later_stages(back_acc)
    hidden = wait((back_act * slope).astype(BF))

    w_dims = ((1,), (1,))
    hid = {0: hidden}
    returned = {}

    def level_after(level):
        return sorted({k | bit for k in level for bit in zbits if bit < (k & -k or zcount)})

    def forward(level):
        return {k: flip(hid[k ^ (k & -k)], "dp", 2 * (k & -k)) for k in level}

    def products(ks):
        lhs = jnp.concatenate([hid[k] for k in ks])
        own = dot(lhs, up_weight, w_dims).astype(BF)
        par = dot(lhs, up_other, w_dims).astype(BF)
        return jnp.where(core == 0, own, par), jnp.where(core == 0, par, own)

    def send_back(ks, mine, got):
        mine = (mine.astype(F32) + got.astype(F32)).astype(BF).reshape(len(ks), rows, -1)
        for n, k in enumerate(ks):
            returned[k] = mine[n] if k == 0 else flip(mine[n], "dp", 2 * k)

    def settle(ks):
        stack = jnp.stack([returned[k] for k in ks])
        order = [
            lax.dynamic_index_in_dim(stack, (zrel >> 1) ^ q, 0, keepdims=False) for q in range(len(ks))
        ]
        for mask in reversed(tbits[1:]):
            n = len(order) // 2
            got = flip(jnp.stack(order[n:]), "tensor", mask)
            order = [(order[i], got[i]) for i in range(n)]
            if mask != tbits[1]:
                order = [(a.astype(F32) + wait(b).astype(F32)).astype(BF) for a, b in order]
        return order[0]

    def add_pair(pair):
        return (pair[0].astype(F32) + wait(pair[1]).astype(F32)).astype(BF)

    first = level_after([0])
    coming = forward(first)
    up_matrix = up_accum[0] + dot(tok_win, hidden, ((0,), (0,))) * scale
    both = dot(up_q, up_matrix, ((0,), (1,)), HIGHEST)
    down_sum = down_sum + wait(down_got)
    down_gram = dot(down_sum, down_sum, ((1,), (1,)), HIGHEST)
    down_term = dot(down_sum, down_matrix, ((1,), (0,)), HIGHEST)
    both = jnp.concatenate([both, down_term, down_gram], axis=1)
    for mask in tbits:
        both = both + wait(flip(both, "tensor", mask))
    both = both + wait(flip(both, "dp", 1))
    for k in reversed(first):
        hid[k] = wait(coming[k])
    group = [0] + first
    level = level_after(first)
    coming = forward(level)
    mine, send = products(group)
    send_got = flip(send, "tensor", 1)
    both_got = flip(both, "dp", dbits[1])
    send_back(group, mine, wait(send_got))
    both = both + wait(both_got)
    for mask in dbits[2:-1]:
        both = both + wait(flip(both, "dp", mask))
    both_got = flip(both, "dp", dbits[-1])
    while level:
        for k in level:
            hid[k] = wait(coming[k])
        mine, send = products(level)
        send_got = flip(send, "tensor", 1)
        after = level_after(level)
        coming = forward(after)
        send_back(level, mine, wait(send_got))
        level = after
    both = both + wait(both_got)
    up_sum, down_term, down_gram = both[:, :window], both[:, window : 2 * window], both[:, 2 * window :]
    up_inv, down_inv = inverse_factors(
        dot(up_sum, up_sum, ((1,), (1,)), HIGHEST), down_gram / replicas
    )

    def scaled(inv, arr):
        return dot(inv, arr, precision=HIGHEST)

    outer = ((0,), (0,))
    up_left = scaled(up_inv, up_sum)
    up_right = dot(up_left, up_matrix, ((1,), (0,)), HIGHEST).astype(BF)
    right_got = flip(up_right, "dp", 1)
    returned.update({k: wait(returned[k]) for k in even[1:]})
    pair_a = settle(even)
    up_right = up_right.astype(F32) + wait(right_got).astype(F32)
    for n, mask in enumerate(dbits[1:]):
        up_right = up_right.astype(BF)
        right_got = flip(up_right, "dp", mask)
        if n == 0:
            returned.update({k: wait(returned[k]) for k in odd})
            pair_b = settle(odd)
        if n == 1:
            sum_a, sum_b = add_pair(pair_a), add_pair(pair_b)
            low = zrel & 1
            got = flip(jnp.where(low == 0, sum_b, sum_a), "tensor", 1)
        up_right = up_right.astype(F32) + wait(right_got).astype(F32)
    own = jnp.where(low == 0, sum_a, sum_b)
    got = wait(got)
    input_grad = jnp.concatenate(
        [jnp.where(half == 0, own, got), jnp.where(half == 0, got, own)], axis=1
    )
    up_right = up_right / replicas
    up_error = up_matrix - dot(up_left, up_right, outer, HIGHEST)
    down_left = scaled(down_inv, down_sum)
    down_right = scaled(down_inv, down_term) / replicas
    down_error = down_matrix - dot(down_left, down_right, outer, HIGHEST)
    up_left, up_right, down_left, down_right = up_left.T, up_right.T, down_left.T, down_right.T
    return (input_grad, up_error[None], up_left, up_right, down_error[None], down_left, down_right)


def solution(mesh):
    return jax.shard_map(
        shards,
        mesh=mesh,
        in_specs=(
            P("dp", "tensor"),
            P("dp", "tensor"),
            P("dp", "tensor"),
            P("tensor", "dp"),
            P("dp", None, "tensor"),
            P("dp", "tensor", None),
            P("tensor", None),
            P(),
        ),
        out_specs=(
            P("dp", "tensor"),
            P("dp", None, "tensor"),
            P(),
            P("tensor", None),
            P("dp", "tensor", None),
            P("tensor", None),
            P(),
        ),
        check_vma=False,
    )
```

```python
import math

import jax
import jax.numpy as jnp
from jax import lax
from jax.experimental import pallas as pl
from jax.experimental.pallas import tpu as pltpu
from jax.sharding import PartitionSpec as P

BF = jnp.bfloat16
F32 = jnp.float32
HIGHEST = lax.Precision.HIGHEST
HIGH = lax.Precision.HIGH


def flip(arr, axis, mask):
    size = lax.axis_size(axis)
    return lax.ppermute(arr, axis, [(i, i ^ mask) for i in range(size)])


def bits_of(size):
    return [1 << b for b in range(size.bit_length() - 1)]


def dot(a, b, dims=((1,), (0,)), precision=None):
    return lax.dot_general(a, b, (dims, ((), ())), preferred_element_type=F32, precision=precision)


def factor_kernel(up_ref, down_ref, up_out, down_out):
    rank = up_ref.shape[0]
    row_id = lax.broadcasted_iota(jnp.int32, (rank, 2 * rank), 0)
    col_id = lax.broadcasted_iota(jnp.int32, (rank, 2 * rank), 1)
    eye = (row_id + rank == col_id).astype(F32)
    state = [
        eye + jnp.concatenate([ref[...], jnp.zeros((rank, rank), F32)], axis=1)
        for ref in (up_ref, down_ref)
    ]
    for j in range(rank):
        for n in range(2):
            aug = state[n]
            root = lax.rsqrt(aug[j : j + 1, j : j + 1])
            row = aug[j : j + 1, :] * root
            col = aug[:, j : j + 1] * root
            state[n] = jnp.where(row_id > j, aug - col * row, jnp.where(row_id == j, row, aug))
    up_out[...] = state[0][:, rank:]
    down_out[...] = state[1][:, rank:]


def inverse_factors(up_gram, down_gram):
    shape = jax.ShapeDtypeStruct(up_gram.shape, F32)
    return pl.pallas_call(
        factor_kernel,
        out_shape=(shape, shape),
        name="inverse_factors",
        cost_estimate=pl.CostEstimate(flops=10**6, bytes_accessed=20000, transcendentals=64),
    )(up_gram, down_gram)


class Order:
    def __init__(self):
        self.last = None

    def __call__(self, arr):
        if self.last is not None:
            arr, self.last = lax.optimization_barrier((arr, self.last))
        self.last = arr
        return arr


def tie(*arrs):
    return lax.optimization_barrier(arrs)


def split_half(arr, half):
    width = arr.shape[1] // 2
    lo, hi = arr[:, :width], arr[:, width:]
    return jnp.where(half == 0, lo, hi), jnp.where(half == 0, hi, lo)


def shards(tokens, out_grad, up_weight, down_weight, up_accum, down_accum, up_q, down_q):
    replicas, columns = lax.axis_size("dp"), lax.axis_size("tensor")
    dp_i, t_i = lax.axis_index("dp"), lax.axis_index("tensor")
    x_i, z_i = dp_i % 2, dp_i // 2
    core = t_i % 2
    zcount = replicas // 2
    zbits, tbits, dbits = bits_of(zcount), bits_of(columns), bits_of(replicas)
    rows = tokens.shape[0]
    window = up_accum.shape[1]
    scale = 1.0 / math.sqrt(rows)
    half = core ^ x_i
    zrel = z_i ^ t_i
    wait = Order()

    def send_z(blocks):
        kept = []
        for k in range(blocks.shape[0]):
            piece = lax.dynamic_index_in_dim(blocks, zrel ^ k, 0, keepdims=False)
            kept.append(piece if k == 0 else flip(piece, "dp", 2 * k))
        return kept

    ucut = (up_weight.shape[0] * 7 // 16 + 31) // 32 * 32
    dcut = (down_weight.shape[0] // 2 + 127) // 128 * 128
    up_a = flip(up_weight[:ucut], "dp", 1)
    mine, swap = split_half(tokens, half)
    tok_blocks = [mine, wait(flip(swap, "tensor", 1))]
    got = flip(jnp.stack(tok_blocks), "tensor", tbits[1])
    grad_in, tok_win, grad_win, wait.last = tie(
        out_grad, tokens[:, :window], out_grad[:, :window], wait.last
    )
    mine, swap = split_half(grad_in, half)
    swap = flip(swap, "tensor", 1)
    windows = jnp.stack([tok_win, grad_win])
    windows = jnp.where(t_i == 0, windows, jnp.zeros_like(windows))
    win_got = lax.ppermute(windows, "tensor", [(0, 1)])
    grad_blocks = [mine, wait(swap)]
    for mask in tbits[1:]:
        if mask > tbits[1]:
            got = flip(jnp.stack(tok_blocks), "tensor", mask)
        got = wait(got)
        tok_blocks = tok_blocks + [got[n] for n in range(len(tok_blocks))]
    tok_keep = send_z(jnp.stack(tok_blocks))
    up_a = wait(up_a)
    up_b_in, up_a = tie(up_weight[ucut:], up_a)
    up_b = flip(up_b_in, "dp", 1)
    grad_got = flip(jnp.stack(grad_blocks), "tensor", tbits[1])
    tok_keep = [tok_keep[0]] + [wait(piece) for piece in tok_keep[1:-1]] + tok_keep[-1:]
    up_b = wait(up_b)
    down_a_in, up_b = tie(down_weight[:dcut], up_b)
    down_a = flip(down_a_in, "dp", 1)
    tok_keep[-1] = wait(tok_keep[-1])
    for mask in tbits[1:]:
        if mask > tbits[1]:
            grad_got = flip(jnp.stack(grad_blocks), "tensor", mask)
        grad_got = wait(grad_got)
        grad_blocks = grad_blocks + [grad_got[n] for n in range(len(grad_blocks))]
    grad_keep = send_z(jnp.stack(grad_blocks))
    tok_other = [wait(flip(piece, "tensor", 1)) for piece in tok_keep]
    up_other = jnp.concatenate([up_a, up_b])

    def other_halves(kept):
        got = [flip(piece, "tensor", 1) for piece in kept]
        return [wait(piece) for piece in got]

    def partial(kept, other, own_w, par_w, dims):
        def part_of(ks):
            a = jnp.concatenate([jnp.where(core == 0, kept[k], other[k]) for k in ks])
            b = jnp.concatenate([jnp.where(core == 0, other[k], kept[k]) for k in ks])
            return (dot(a, own_w, dims) + dot(b, par_w, dims)).reshape(len(ks), rows, -1)

        return part_of

    odd = [k for k in range(zcount) if k & 1]
    even = [k for k in range(zcount) if not k & 1]

    def later_stages(acc):
        ks = even
        for bit in zbits[1:]:
            sel = [n for n, k in enumerate(ks) if k & bit]
            stay = [n for n, k in enumerate(ks) if not k & bit]
            send = jnp.stack([acc[n] for n in sel]).astype(BF)
            acc = jnp.stack([acc[n] for n in stay]) + wait(flip(send, "dp", 2 * bit)).astype(F32)
            ks = [ks[n] for n in stay]
        return acc[0]

    part_of = partial(tok_keep, tok_other, up_weight, up_other, ((1,), (0,)))
    pre_got = flip(part_of(odd).astype(BF), "dp", 2)
    pre_acc = part_of(even)
    grad_keep = [grad_keep[0]] + [wait(piece) for piece in grad_keep[1:]]
    pre_acc = pre_acc + wait(pre_got).astype(F32)
    down_a = wait(down_a)
    down_b_in, down_a = tie(down_weight[dcut:], down_a)
    down_b = flip(down_b_in, "dp", 1)
    windows = windows + wait(win_got)
    for n, mask in enumerate(tbits[1:]):
        win_got = lax.ppermute(windows, "tensor", [(i, i + mask) for i in range(mask)])
        if n == 0:
            grad_other = other_halves(grad_keep)
        windows = windows + wait(win_got)
    tok_win, grad_win = windows[0], windows[1]
    down_b = wait(down_b)
    down_other = jnp.concatenate([down_a, down_b])
    part_of = partial(grad_keep, grad_other, down_weight, down_other, ((1,), (1,)))
    back_got = flip(part_of(odd).astype(BF), "dp", 2)
    back_acc = part_of(even)
    preact = later_stages(pre_acc)

    squash = jax.nn.sigmoid(preact)
    act_out = (preact * squash).astype(BF)
    slope = squash * (1.0 + preact * (1.0 - squash))
    down_matrix = down_accum[0] + dot(act_out, grad_win, ((0,), (0,))) * scale
    down_sum = dot(down_q, down_matrix, ((0,), (1,)), HIGH)
    down_got = flip(down_sum, "dp", 1)
    back_acc = back_acc + wait(back_got).astype(F32)
    down_sum = down_sum + wait(down_got)
    for mask in dbits[1:-1]:
        down_sum = down_sum + wait(flip(down_sum, "dp", mask))
    down_got = flip(down_sum, "dp", dbits[-1])
    back_act = later_stages(back_acc)
    hidden = wait((back_act * slope).astype(BF))

    w_dims = ((1,), (1,))
    hid = {0: hidden}
    returned = {}

    def level_after(level):
        return sorted({k | bit for k in level for bit in zbits if bit < (k & -k or zcount)})

    def forward(level):
        return {k: flip(hid[k ^ (k & -k)], "dp", 2 * (k & -k)) for k in level}

    def start_back(k):
        own = dot(hid[k], up_weight, w_dims).astype(BF)
        par = dot(hid[k], up_other, w_dims).astype(BF)
        return jnp.where(core == 0, own, par), flip(jnp.where(core == 0, par, own), "tensor", 1)

    def send_back(k, mine, got):
        mine = (mine.astype(F32) + got.astype(F32)).astype(BF)
        returned[k] = mine if k == 0 else flip(mine, "dp", 2 * k)

    def settle(ks):
        stack = jnp.stack([returned[k] for k in ks])
        order = [
            lax.dynamic_index_in_dim(stack, (zrel >> 1) ^ q, 0, keepdims=False) for q in range(len(ks))
        ]
        for mask in reversed(tbits[1:]):
            n = len(order) // 2
            got = flip(jnp.stack(order[n:]), "tensor", mask)
            order = [(order[i], got[i]) for i in range(n)]
            if mask != tbits[1]:
                order = [(a.astype(F32) + wait(b).astype(F32)).astype(BF) for a, b in order]
        return order[0]

    def add_pair(pair):
        return (pair[0].astype(F32) + wait(pair[1]).astype(F32)).astype(BF)

    first = level_after([0])
    coming = forward(first)
    up_matrix = up_accum[0] + dot(tok_win, hidden, ((0,), (0,))) * scale
    both = dot(up_q, up_matrix, ((0,), (1,)), HIGH)
    down_sum = down_sum + wait(down_got)
    down_gram = dot(down_sum, down_sum, ((1,), (1,)), HIGHEST)
    down_term = dot(down_sum, down_matrix, ((1,), (0,)), HIGH)
    both = jnp.concatenate([both, down_term, down_gram], axis=1)
    both = both + wait(flip(both, "tensor", 1))
    both_got = flip(both, "tensor", tbits[1])
    mine, got = start_back(0)
    send_back(0, mine, wait(got))
    for k in reversed(first):
        hid[k] = wait(coming[k])
    level = level_after(first)
    coming = forward(level)
    both = both + wait(both_got)
    for mask in tbits[2:]:
        both = both + wait(flip(both, "tensor", mask))
    both_got = flip(both, "dp", 1)
    pending = {k: start_back(k) for k in first}
    both = both + wait(both_got)
    both_got = flip(both, "dp", dbits[1])
    for k in first:
        mine, got = pending[k]
        send_back(k, mine, wait(got))
    for k in level:
        hid[k] = wait(coming[k])
    pending = {k: start_back(k) for k in level}
    after = level_after(level)
    coming = forward(after)
    for mask in dbits[2:]:
        both = both + wait(both_got)
        both_got = flip(both, "dp", mask)
    for k in level:
        mine, got = pending[k]
        send_back(k, mine, wait(got))
    both = both + wait(both_got)
    up_sum, down_term, down_gram = both[:, :window], both[:, window : 2 * window], both[:, 2 * window :]
    up_inv, down_inv = inverse_factors(
        dot(up_sum, up_sum, ((1,), (1,)), HIGHEST), down_gram / replicas
    )

    def scaled(inv, arr):
        return dot(inv, arr, precision=HIGHEST)

    outer = ((0,), (0,))
    up_left = scaled(up_inv, up_sum)
    up_right = dot(up_left, up_matrix, ((1,), (0,)), HIGH).astype(BF)
    right_got = flip(up_right, "dp", 1)
    level = after
    while level:
        for k in level:
            hid[k] = wait(coming[k])
        after = level_after(level)
        coming = forward(after)
        for k in level:
            mine, got = start_back(k)
            send_back(k, mine, wait(got))
        level = after
    returned.update({k: wait(returned[k]) for k in even[1:]})
    pair_a = settle(even)
    returned.update({k: wait(returned[k]) for k in odd})
    pair_b = settle(odd)
    up_right = up_right.astype(F32) + wait(right_got).astype(F32)
    for n, mask in enumerate(dbits[1:]):
        up_right = up_right.astype(BF)
        right_got = flip(up_right, "dp", mask)
        if n == 0:
            sum_a, sum_b = add_pair(pair_a), add_pair(pair_b)
            low = zrel & 1
            got = flip(jnp.where(low == 0, sum_b, sum_a), "tensor", 1)
        if n == 1:
            got = wait(got)
        up_right = up_right.astype(F32) + wait(right_got).astype(F32)
    own = jnp.where(low == 0, sum_a, sum_b)
    input_grad = jnp.concatenate(
        [jnp.where(half == 0, own, got), jnp.where(half == 0, got, own)], axis=1
    )
    up_right = up_right / replicas
    up_error = up_matrix - dot(up_left, up_right, outer, HIGH)
    down_left = scaled(down_inv, down_sum)
    down_right = scaled(down_inv, down_term) / replicas
    down_error = down_matrix - dot(down_left, down_right, outer, HIGH)
    up_left, up_right, down_left, down_right = up_left.T, up_right.T, down_left.T, down_right.T
    return (input_grad, up_error[None], up_left, up_right, down_error[None], down_left, down_right)


def solution(mesh):
    return jax.shard_map(
        shards,
        mesh=mesh,
        in_specs=(
            P("dp", "tensor"),
            P("dp", "tensor"),
            P("dp", "tensor"),
            P("tensor", "dp"),
            P("dp", None, "tensor"),
            P("dp", "tensor", None),
            P("tensor", None),
            P(),
        ),
        out_specs=(
            P("dp", "tensor"),
            P("dp", None, "tensor"),
            P(),
            P("tensor", None),
            P("dp", "tensor", None),
            P("tensor", None),
            P(),
        ),
        check_vma=False,
    )
```

```python
import functools
import math

import jax
import jax.numpy as jnp
from jax import lax
from jax.experimental import pallas as pl
from jax.experimental.pallas import tpu as pltpu
from jax.sharding import PartitionSpec as P

BF = jnp.bfloat16
F32 = jnp.float32
HIGHEST = lax.Precision.HIGHEST
HIGH = lax.Precision.HIGH


def flip(arr, axis, mask):
    size = lax.axis_size(axis)
    return lax.ppermute(arr, axis, [(i, i ^ mask) for i in range(size)])


def bits_of(size):
    return [1 << b for b in range(size.bit_length() - 1)]


def dot(a, b, dims=((1,), (0,)), precision=None):
    return lax.dot_general(a, b, (dims, ((), ())), preferred_element_type=F32, precision=precision)


def factor_kernel(replicas, sums_ref, left_out, down_out):
    rank = down_out.shape[0]
    window = left_out.shape[1]
    up_sum = sums_ref[:, :window]
    grams = (
        dot(up_sum, up_sum, ((1,), (1,)), HIGHEST),
        sums_ref[:, 2 * window :] * (1.0 / replicas),
    )
    row_id = lax.broadcasted_iota(jnp.int32, (rank, 2 * rank), 0)
    col_id = lax.broadcasted_iota(jnp.int32, (rank, 2 * rank), 1)
    eye = (row_id + rank == col_id).astype(F32)
    state = [
        eye + jnp.concatenate([gram, jnp.zeros((rank, rank), F32)], axis=1) for gram in grams
    ]
    for j in range(rank):
        for n in range(2):
            aug = state[n]
            root = lax.rsqrt(aug[j : j + 1, j : j + 1])
            row = aug[j : j + 1, :] * root
            col = aug[:, j : j + 1] * root
            state[n] = jnp.where(row_id > j, aug - col * row, jnp.where(row_id == j, row, aug))
    left_out[...] = dot(state[0][:, rank:], up_sum, precision=HIGHEST)
    down_out[...] = state[1][:, rank:]


def factors(sums, window, replicas):
    rank = sums.shape[0]
    return pl.pallas_call(
        functools.partial(factor_kernel, replicas),
        out_shape=(
            jax.ShapeDtypeStruct((rank, window), F32),
            jax.ShapeDtypeStruct((rank, rank), F32),
        ),
        name="factors",
        cost_estimate=pl.CostEstimate(flops=10**6, bytes_accessed=20000, transcendentals=64),
    )(sums)


class Order:
    def __init__(self):
        self.last = None

    def __call__(self, arr):
        if self.last is not None:
            arr, self.last = lax.optimization_barrier((arr, self.last))
        self.last = arr
        return arr


def tie(*arrs):
    return lax.optimization_barrier(arrs)


def split_half(arr, half):
    width = arr.shape[1] // 2
    lo, hi = arr[:, :width], arr[:, width:]
    return jnp.where(half == 0, lo, hi), jnp.where(half == 0, hi, lo)


def shards(tokens, out_grad, up_weight, down_weight, up_accum, down_accum, up_q, down_q):
    replicas, columns = lax.axis_size("dp"), lax.axis_size("tensor")
    dp_i, t_i = lax.axis_index("dp"), lax.axis_index("tensor")
    x_i, z_i = dp_i % 2, dp_i // 2
    core = t_i % 2
    zcount = replicas // 2
    zbits, tbits, dbits = bits_of(zcount), bits_of(columns), bits_of(replicas)
    rows = tokens.shape[0]
    window = up_accum.shape[1]
    scale = 1.0 / math.sqrt(rows)
    half = core ^ x_i
    zrel = z_i ^ t_i
    wait = Order()

    def send_z(blocks):
        kept = []
        for k in range(blocks.shape[0]):
            piece = lax.dynamic_index_in_dim(blocks, zrel ^ k, 0, keepdims=False)
            kept.append(piece if k == 0 else flip(piece, "dp", 2 * k))
        return kept

    ucut = (up_weight.shape[0] * 7 // 16 + 31) // 32 * 32
    dcut = (down_weight.shape[0] // 2 + 127) // 128 * 128
    up_a = flip(up_weight[:ucut], "dp", 1)
    mine, swap = split_half(tokens, half)
    tok_blocks = [mine, wait(flip(swap, "tensor", 1))]
    got = flip(jnp.stack(tok_blocks), "tensor", tbits[1])
    grad_in, tok_win, grad_win, wait.last = tie(
        out_grad, tokens[:, :window], out_grad[:, :window], wait.last
    )
    mine, swap = split_half(grad_in, half)
    swap = flip(swap, "tensor", 1)
    windows = jnp.stack([tok_win, grad_win])
    windows = jnp.where(t_i == 0, windows, jnp.zeros_like(windows))
    win_got = lax.ppermute(windows, "tensor", [(0, 1)])
    grad_blocks = [mine, wait(swap)]
    for mask in tbits[1:]:
        if mask > tbits[1]:
            got = flip(jnp.stack(tok_blocks), "tensor", mask)
        got = wait(got)
        tok_blocks = tok_blocks + [got[n] for n in range(len(tok_blocks))]
    tok_keep = send_z(jnp.stack(tok_blocks))
    up_a = wait(up_a)
    up_b_in, up_a = tie(up_weight[ucut:], up_a)
    up_b = flip(up_b_in, "dp", 1)
    grad_got = flip(jnp.stack(grad_blocks), "tensor", tbits[1])
    tok_keep = [tok_keep[0]] + [wait(piece) for piece in tok_keep[1:-1]] + tok_keep[-1:]
    up_b = wait(up_b)
    down_a_in, up_b = tie(down_weight[:dcut], up_b)
    down_a = flip(down_a_in, "dp", 1)
    tok_keep[-1] = wait(tok_keep[-1])
    for mask in tbits[1:]:
        if mask > tbits[1]:
            grad_got = flip(jnp.stack(grad_blocks), "tensor", mask)
        grad_got = wait(grad_got)
        grad_blocks = grad_blocks + [grad_got[n] for n in range(len(grad_blocks))]
    grad_keep = send_z(jnp.stack(grad_blocks))
    tok_other = [wait(flip(piece, "tensor", 1)) for piece in tok_keep]
    up_other = jnp.concatenate([up_a, up_b])

    def other_halves(kept):
        got = [flip(piece, "tensor", 1) for piece in kept]
        return [wait(piece) for piece in got]

    def partial(kept, other, own_w, par_w, dims):
        def part_of(ks):
            a = jnp.concatenate([jnp.where(core == 0, kept[k], other[k]) for k in ks])
            b = jnp.concatenate([jnp.where(core == 0, other[k], kept[k]) for k in ks])
            return (dot(a, own_w, dims) + dot(b, par_w, dims)).reshape(len(ks), rows, -1)

        return part_of

    odd = [k for k in range(zcount) if k & 1]
    even = [k for k in range(zcount) if not k & 1]

    def later_stages(acc):
        ks = even
        for bit in zbits[1:]:
            sel = [n for n, k in enumerate(ks) if k & bit]
            stay = [n for n, k in enumerate(ks) if not k & bit]
            send = jnp.stack([acc[n] for n in sel]).astype(BF)
            acc = jnp.stack([acc[n] for n in stay]) + wait(flip(send, "dp", 2 * bit)).astype(F32)
            ks = [ks[n] for n in stay]
        return acc[0]

    part_of = partial(tok_keep, tok_other, up_weight, up_other, ((1,), (0,)))
    pre_got = flip(part_of(odd).astype(BF), "dp", 2)
    pre_acc = part_of(even)
    grad_keep = [grad_keep[0]] + [wait(piece) for piece in grad_keep[1:]]
    pre_acc = pre_acc + wait(pre_got).astype(F32)
    down_a = wait(down_a)
    down_b_in, down_a = tie(down_weight[dcut:], down_a)
    down_b = flip(down_b_in, "dp", 1)
    windows = windows + wait(win_got)
    for n, mask in enumerate(tbits[1:]):
        win_got = lax.ppermute(windows, "tensor", [(i, i + mask) for i in range(mask)])
        if n == 0:
            grad_other = other_halves(grad_keep)
        windows = windows + wait(win_got)
    tok_win, grad_win = windows[0], windows[1]
    down_b = wait(down_b)
    down_other = jnp.concatenate([down_a, down_b])
    part_of = partial(grad_keep, grad_other, down_weight, down_other, ((1,), (1,)))
    back_got = flip(part_of(odd).astype(BF), "dp", 2)
    back_acc = part_of(even)
    preact = later_stages(pre_acc)

    squash = jax.nn.sigmoid(preact)
    act_out = (preact * squash).astype(BF)
    slope = squash * (1.0 + preact * (1.0 - squash))
    down_matrix = down_accum[0] + dot(act_out, grad_win, ((0,), (0,))) * scale
    down_sum = dot(down_q, down_matrix, ((0,), (1,)), HIGH)
    down_sum = down_sum.astype(BF)
    down_got = flip(down_sum, "dp", 1)
    back_acc = back_acc + wait(back_got).astype(F32)
    slope, back_acc = tie(slope, back_acc)
    down_sum = down_sum.astype(F32) + wait(down_got).astype(F32)
    for mask in dbits[1:-1]:
        down_sum = down_sum.astype(BF)
        down_sum = down_sum.astype(F32) + wait(flip(down_sum, "dp", mask)).astype(F32)
    down_sum = down_sum.astype(BF)
    down_got = flip(down_sum, "dp", dbits[-1])
    back_act = later_stages(back_acc)
    hidden = wait((back_act * slope).astype(BF))

    w_dims = ((1,), (1,))
    hid = {0: hidden}
    returned = {}

    def level_after(level):
        return sorted({k | bit for k in level for bit in zbits if bit < (k & -k or zcount)})

    def forward(level):
        return {k: flip(hid[k ^ (k & -k)], "dp", 2 * (k & -k)) for k in level}

    def start_back(k):
        own = dot(hid[k], up_weight, w_dims).astype(BF)
        par = dot(hid[k], up_other, w_dims).astype(BF)
        return jnp.where(core == 0, own, par), flip(jnp.where(core == 0, par, own), "tensor", 1)

    def send_back(k, mine, got):
        mine = (mine.astype(F32) + got.astype(F32)).astype(BF)
        returned[k] = mine if k == 0 else flip(mine, "dp", 2 * k)

    def settle(ks):
        stack = jnp.stack([returned[k] for k in ks])
        order = [
            lax.dynamic_index_in_dim(stack, (zrel >> 1) ^ q, 0, keepdims=False) for q in range(len(ks))
        ]
        for mask in reversed(tbits[1:]):
            n = len(order) // 2
            got = flip(jnp.stack(order[n:]), "tensor", mask)
            order = [(order[i], got[i]) for i in range(n)]
            if mask != tbits[1]:
                order = [(a.astype(F32) + wait(b).astype(F32)).astype(BF) for a, b in order]
        return order[0]

    def add_pair(pair):
        return (pair[0].astype(F32) + wait(pair[1]).astype(F32)).astype(BF)

    first = level_after([0])
    coming = forward(first)
    up_matrix = up_accum[0] + dot(tok_win, hidden, ((0,), (0,))) * scale
    both = dot(up_q, up_matrix, ((0,), (1,)), HIGH)
    down_sum = down_sum.astype(F32) + wait(down_got).astype(F32)
    down_gram = dot(down_sum, down_sum, ((1,), (1,)), HIGHEST)
    down_term = dot(down_sum, down_matrix, ((1,), (0,)), HIGH)
    both = jnp.concatenate([both, down_term, down_gram], axis=1)
    both = both + wait(flip(both, "tensor", 1))
    both_got = flip(both, "tensor", tbits[1])
    mine, got = start_back(0)
    send_back(0, mine, wait(got))
    for k in reversed(first):
        hid[k] = wait(coming[k])
    level = level_after(first)
    coming = forward(level)
    both = both + wait(both_got)
    for mask in tbits[2:]:
        both = both + wait(flip(both, "tensor", mask))
    both_got = flip(both, "dp", 1)
    pending = {k: start_back(k) for k in first}
    both = both + wait(both_got)
    both_got = flip(both, "dp", dbits[1])
    for k in first:
        mine, got = pending[k]
        send_back(k, mine, wait(got))
    for k in level:
        hid[k] = wait(coming[k])
    pending = {k: start_back(k) for k in level}
    after = level_after(level)
    coming = forward(after)
    for mask in dbits[2:]:
        both = both + wait(both_got)
        both_got = flip(both, "dp", mask)
    for k in level:
        mine, got = pending[k]
        send_back(k, mine, wait(got))
    both = both + wait(both_got)
    down_term = both[:, window : 2 * window]
    up_left, down_inv = factors(both, window, replicas)

    def scaled(inv, arr):
        return dot(inv, arr, precision=HIGHEST)

    outer = ((0,), (0,))
    up_right = dot(up_left, up_matrix, ((1,), (0,)), HIGH).astype(BF)
    right_got = flip(up_right, "dp", 1)
    level = after
    while level:
        for k in level:
            hid[k] = wait(coming[k])
        after = level_after(level)
        coming = forward(after)
        for k in level:
            mine, got = start_back(k)
            send_back(k, mine, wait(got))
        level = after
    returned.update({k: wait(returned[k]) for k in even[1:]})
    pair_a = settle(even)
    up_right = up_right.astype(F32) + wait(right_got).astype(F32)
    down_inv, wait.last = tie(down_inv, wait.last)
    low = zrel & 1
    for n, mask in enumerate(dbits[1:]):
        up_right = up_right.astype(BF)
        right_got = flip(up_right, "dp", mask)
        if n == 0:
            returned.update({k: wait(returned[k]) for k in odd})
            pair_b = settle(odd)
        if n == 1:
            sum_a, sum_b = add_pair(pair_a), add_pair(pair_b)
            got = flip(jnp.where(low == 0, sum_b, sum_a), "tensor", 1)
        up_right = up_right.astype(F32) + wait(right_got).astype(F32)
    own = jnp.where(low == 0, sum_a, sum_b)
    got = wait(got)
    input_grad = jnp.concatenate(
        [jnp.where(half == 0, own, got), jnp.where(half == 0, got, own)], axis=1
    )
    up_right = up_right / replicas
    up_error = up_matrix - dot(up_left, up_right, outer, HIGH)
    down_left = scaled(down_inv, down_sum)
    down_right = scaled(down_inv, down_term) / replicas
    down_error = down_matrix - dot(down_left, down_right, outer, HIGH)
    up_left, up_right, down_left, down_right = up_left.T, up_right.T, down_left.T, down_right.T
    return (input_grad, up_error[None], up_left, up_right, down_error[None], down_left, down_right)


def solution(mesh):
    return jax.shard_map(
        shards,
        mesh=mesh,
        in_specs=(
            P("dp", "tensor"),
            P("dp", "tensor"),
            P("dp", "tensor"),
            P("tensor", "dp"),
            P("dp", None, "tensor"),
            P("dp", "tensor", None),
            P("tensor", None),
            P(),
        ),
        out_specs=(
            P("dp", "tensor"),
            P("dp", None, "tensor"),
            P(),
            P("tensor", None),
            P("dp", "tensor", None),
            P("tensor", None),
            P(),
        ),
        check_vma=False,
    )
```

```python
import functools
import math

import jax
import jax.numpy as jnp
from jax import lax
from jax.experimental import pallas as pl
from jax.experimental.pallas import tpu as pltpu
from jax.sharding import PartitionSpec as P

BF = jnp.bfloat16
F32 = jnp.float32
HIGHEST = lax.Precision.HIGHEST
HIGH = lax.Precision.HIGH


def flip(arr, axis, mask):
    size = lax.axis_size(axis)
    return lax.ppermute(arr, axis, [(i, i ^ mask) for i in range(size)])


def bits_of(size):
    return [1 << b for b in range(size.bit_length() - 1)]


def dot(a, b, dims=((1,), (0,)), precision=None):
    return lax.dot_general(a, b, (dims, ((), ())), preferred_element_type=F32, precision=precision)


def factor_kernel(replicas, sums_ref, left_out, down_out):
    rank = down_out.shape[0]
    window = left_out.shape[1]
    up_sum = sums_ref[:, :window]
    grams = (
        dot(up_sum, up_sum, ((1,), (1,)), HIGHEST),
        sums_ref[:, 2 * window :] * (1.0 / replicas),
    )
    row_id = lax.broadcasted_iota(jnp.int32, (rank, 2 * rank), 0)
    col_id = lax.broadcasted_iota(jnp.int32, (rank, 2 * rank), 1)
    eye = (row_id + rank == col_id).astype(F32)
    state = [
        eye + jnp.concatenate([gram, jnp.zeros((rank, rank), F32)], axis=1) for gram in grams
    ]
    for j in range(rank):
        for n in range(2):
            aug = state[n]
            root = lax.rsqrt(aug[j : j + 1, j : j + 1])
            row = aug[j : j + 1, :] * root
            col = aug[:, j : j + 1] * root
            state[n] = jnp.where(row_id > j, aug - col * row, jnp.where(row_id == j, row, aug))
    left_out[...] = dot(state[0][:, rank:], up_sum, precision=HIGHEST)
    down_out[...] = state[1][:, rank:]


def factors(sums, window, replicas):
    rank = sums.shape[0]
    return pl.pallas_call(
        functools.partial(factor_kernel, replicas),
        out_shape=(
            jax.ShapeDtypeStruct((rank, window), F32),
            jax.ShapeDtypeStruct((rank, rank), F32),
        ),
        name="factors",
        cost_estimate=pl.CostEstimate(flops=10**6, bytes_accessed=20000, transcendentals=64),
    )(sums)


class Order:
    def __init__(self):
        self.last = None

    def __call__(self, arr):
        if self.last is not None:
            arr, self.last = lax.optimization_barrier((arr, self.last))
        self.last = arr
        return arr


def tie(*arrs):
    return lax.optimization_barrier(arrs)


def split_half(arr, half):
    width = arr.shape[1] // 2
    lo, hi = arr[:, :width], arr[:, width:]
    return jnp.where(half == 0, lo, hi), jnp.where(half == 0, hi, lo)


def shards(tokens, out_grad, up_weight, down_weight, up_accum, down_accum, up_q, down_q):
    replicas, columns = lax.axis_size("dp"), lax.axis_size("tensor")
    dp_i, t_i = lax.axis_index("dp"), lax.axis_index("tensor")
    x_i, z_i = dp_i % 2, dp_i // 2
    core = t_i % 2
    zcount = replicas // 2
    zbits, tbits, dbits = bits_of(zcount), bits_of(columns), bits_of(replicas)
    rows = tokens.shape[0]
    window = up_accum.shape[1]
    scale = 1.0 / math.sqrt(rows)
    half = core ^ x_i
    zrel = z_i ^ t_i
    wait = Order()

    def send_z(blocks):
        kept = []
        for k in range(blocks.shape[0]):
            piece = lax.dynamic_index_in_dim(blocks, zrel ^ k, 0, keepdims=False)
            kept.append(piece if k == 0 else flip(piece, "dp", 2 * k))
        return kept

    ucut = (up_weight.shape[0] * 7 // 16 + 31) // 32 * 32
    dcut = (down_weight.shape[0] * 2 // 3 + 127) // 128 * 128
    up_a = flip(up_weight[:ucut], "dp", 1)
    mine, swap = split_half(tokens, half)
    tok_blocks = [mine, wait(flip(swap, "tensor", 1))]
    got = flip(jnp.stack(tok_blocks), "tensor", tbits[1])
    grad_in, wait.last = tie(out_grad, wait.last)
    mine, swap = split_half(grad_in, half)
    swap = flip(swap, "tensor", 1)
    grad_blocks = [mine, wait(swap)]
    for mask in tbits[1:]:
        if mask > tbits[1]:
            got = flip(jnp.stack(tok_blocks), "tensor", mask)
        got = wait(got)
        tok_blocks = tok_blocks + [got[n] for n in range(len(tok_blocks))]
    tok_blocks = jnp.stack(tok_blocks)
    tok_keep = send_z(tok_blocks)
    up_a = wait(up_a)
    up_b_in, up_a = tie(up_weight[ucut:], up_a)
    up_b = flip(up_b_in, "dp", 1)
    grad_got = flip(jnp.stack(grad_blocks), "tensor", tbits[1])
    tok_keep = [tok_keep[0]] + [wait(piece) for piece in tok_keep[1:-1]] + tok_keep[-1:]
    up_b = wait(up_b)
    down_a_in, up_b = tie(down_weight[:dcut], up_b)
    down_a = flip(down_a_in, "dp", 1)
    tok_keep[-1] = wait(tok_keep[-1])
    for mask in tbits[1:]:
        if mask > tbits[1]:
            grad_got = flip(jnp.stack(grad_blocks), "tensor", mask)
        grad_got = wait(grad_got)
        grad_blocks = grad_blocks + [grad_got[n] for n in range(len(grad_blocks))]
    grad_blocks = jnp.stack(grad_blocks)
    grad_keep = send_z(grad_blocks)
    tok_other = [wait(flip(piece, "tensor", 1)) for piece in tok_keep]
    up_other = jnp.concatenate([up_a, up_b])

    def other_halves(kept):
        got = [flip(piece, "tensor", 1) for piece in kept]
        return [wait(piece) for piece in got]

    def partial(kept, other, own_w, par_w, dims):
        def part_of(ks):
            a = jnp.concatenate([jnp.where(core == 0, kept[k], other[k]) for k in ks])
            b = jnp.concatenate([jnp.where(core == 0, other[k], kept[k]) for k in ks])
            return (dot(a, own_w, dims) + dot(b, par_w, dims)).reshape(len(ks), rows, -1)

        return part_of

    odd = [k for k in range(zcount) if k & 1]
    even = [k for k in range(zcount) if not k & 1]

    def later_stages(acc):
        ks = even
        for bit in zbits[1:]:
            sel = [n for n, k in enumerate(ks) if k & bit]
            stay = [n for n, k in enumerate(ks) if not k & bit]
            send = jnp.stack([acc[n] for n in sel]).astype(BF)
            acc = jnp.stack([acc[n] for n in stay]) + wait(flip(send, "dp", 2 * bit)).astype(F32)
            ks = [ks[n] for n in stay]
        return acc[0]

    part_of = partial(tok_keep, tok_other, up_weight, up_other, ((1,), (0,)))
    pre_got = flip(part_of(odd).astype(BF), "dp", 2)
    pre_acc = part_of(even)
    grad_keep = [grad_keep[0]] + [wait(piece) for piece in grad_keep[1:]]
    pre_acc = pre_acc + wait(pre_got).astype(F32)
    down_a = wait(down_a)
    down_b_in, down_a = tie(down_weight[dcut:], down_a)
    down_b = flip(down_b_in, "dp", 1)
    if 2 * window <= tokens.shape[1]:
        windows = jnp.stack(
            [
                lax.dynamic_index_in_dim(blocks, t_i, 0, keepdims=False)[:, :window]
                for blocks in (tok_blocks, grad_blocks)
            ]
        )
        windows = jnp.where(half == 0, windows, wait(flip(windows, "tensor", 1)))
    else:
        windows = jnp.stack([tokens[:, :window], out_grad[:, :window]])
        windows = jnp.where(t_i == 0, windows, jnp.zeros_like(windows))
        for mask in tbits:
            windows = windows + wait(
                lax.ppermute(windows, "tensor", [(i, i + mask) for i in range(mask)])
            )
    tok_win, grad_win = windows[0], windows[1]
    grad_other = other_halves(grad_keep)
    down_b = wait(down_b)
    down_other = jnp.concatenate([down_a, down_b])
    part_of = partial(grad_keep, grad_other, down_weight, down_other, ((1,), (1,)))
    back_got = flip(part_of(odd).astype(BF), "dp", 2)
    back_acc = part_of(even)
    preact = later_stages(pre_acc)

    squash = jax.nn.sigmoid(preact)
    act_out = (preact * squash).astype(BF)
    slope = squash * (1.0 + preact * (1.0 - squash))
    down_matrix = down_accum[0] + dot(act_out, grad_win, ((0,), (0,))) * scale
    down_sum = dot(down_q, down_matrix, ((0,), (1,)), HIGH)
    down_sum = down_sum.astype(BF)
    down_got = flip(down_sum, "dp", 1)
    back_acc = back_acc + wait(back_got).astype(F32)
    slope, back_acc = tie(slope, back_acc)
    down_sum = down_sum.astype(F32) + wait(down_got).astype(F32)
    for mask in dbits[1:-1]:
        down_sum = down_sum.astype(BF)
        down_sum = down_sum.astype(F32) + wait(flip(down_sum, "dp", mask)).astype(F32)
    down_sum = down_sum.astype(BF)
    down_got = flip(down_sum, "dp", dbits[-1])
    back_act = later_stages(back_acc)
    hidden = wait((back_act * slope).astype(BF))

    w_dims = ((1,), (1,))
    hid = {0: hidden}
    returned = {}

    def level_after(level):
        return sorted({k | bit for k in level for bit in zbits if bit < (k & -k or zcount)})

    def forward(level):
        return {k: flip(hid[k ^ (k & -k)], "dp", 2 * (k & -k)) for k in level}

    def start_back(k):
        own = dot(hid[k], up_weight, w_dims).astype(BF)
        par = dot(hid[k], up_other, w_dims).astype(BF)
        return jnp.where(core == 0, own, par), flip(jnp.where(core == 0, par, own), "tensor", 1)

    def send_back(k, mine, got):
        mine = (mine.astype(F32) + got.astype(F32)).astype(BF)
        returned[k] = mine if k == 0 else flip(mine, "dp", 2 * k)

    def settle(ks):
        stack = jnp.stack([returned[k] for k in ks])
        order = [
            lax.dynamic_index_in_dim(stack, (zrel >> 1) ^ q, 0, keepdims=False) for q in range(len(ks))
        ]
        for mask in reversed(tbits[1:]):
            n = len(order) // 2
            got = flip(jnp.stack(order[n:]), "tensor", mask)
            order = [(order[i], got[i]) for i in range(n)]
            if mask != tbits[1]:
                order = [(a.astype(F32) + wait(b).astype(F32)).astype(BF) for a, b in order]
        return order[0]

    def add_pair(pair):
        return (pair[0].astype(F32) + wait(pair[1]).astype(F32)).astype(BF)

    first = level_after([0])
    coming = forward(first)
    up_matrix = up_accum[0] + dot(tok_win, hidden, ((0,), (0,))) * scale
    both = dot(up_q, up_matrix, ((0,), (1,)), HIGH)
    down_sum = down_sum.astype(F32) + wait(down_got).astype(F32)
    down_gram = dot(down_sum, down_sum, ((1,), (1,)), HIGHEST)
    down_term = dot(down_sum, down_matrix, ((1,), (0,)), HIGH)
    both = jnp.concatenate([both, down_term, down_gram], axis=1)
    both = both + wait(flip(both, "tensor", 1))
    both_got = flip(both, "tensor", tbits[1])
    mine, got = start_back(0)
    send_back(0, mine, wait(got))
    for k in reversed(first):
        hid[k] = wait(coming[k])
    level = level_after(first)
    coming = forward(level)
    both = both + wait(both_got)
    for mask in tbits[2:]:
        both = both + wait(flip(both, "tensor", mask))
    both_got = flip(both, "dp", 1)
    pending = {k: start_back(k) for k in first}
    both = both + wait(both_got)
    both_got = flip(both, "dp", dbits[1])
    for k in first:
        mine, got = pending[k]
        send_back(k, mine, wait(got))
    for k in level:
        hid[k] = wait(coming[k])
    pending = {k: start_back(k) for k in level}
    after = level_after(level)
    coming = forward(after)
    for mask in dbits[2:]:
        both = both + wait(both_got)
        both_got = flip(both, "dp", mask)
    for k in level:
        mine, got = pending[k]
        send_back(k, mine, wait(got))
    both = both + wait(both_got)
    down_term = both[:, window : 2 * window]
    up_left, down_inv = factors(both, window, replicas)

    def scaled(inv, arr):
        return dot(inv, arr, precision=HIGHEST)

    outer = ((0,), (0,))
    up_right = dot(up_left, up_matrix, ((1,), (0,)), HIGH).astype(BF)
    right_got = flip(up_right, "dp", 1)
    level = after
    while level:
        for k in level:
            hid[k] = wait(coming[k])
        after = level_after(level)
        coming = forward(after)
        for k in level:
            mine, got = start_back(k)
            send_back(k, mine, wait(got))
        level = after
    returned.update({k: wait(returned[k]) for k in even[1:]})
    pair_a = settle(even)
    up_right = up_right.astype(F32) + wait(right_got).astype(F32)
    down_inv, wait.last = tie(down_inv, wait.last)
    low = zrel & 1
    for n, mask in enumerate(dbits[1:]):
        up_right = up_right.astype(BF)
        right_got = flip(up_right, "dp", mask)
        if n == 0:
            returned.update({k: wait(returned[k]) for k in odd})
            pair_b = settle(odd)
        if n == 1:
            sum_a, sum_b = add_pair(pair_a), add_pair(pair_b)
            got = flip(jnp.where(low == 0, sum_b, sum_a), "tensor", 1)
        up_right = up_right.astype(F32) + wait(right_got).astype(F32)
    own = jnp.where(low == 0, sum_a, sum_b)
    got = wait(got)
    input_grad = jnp.concatenate(
        [jnp.where(half == 0, own, got), jnp.where(half == 0, got, own)], axis=1
    )
    up_right = up_right / replicas
    up_error = up_matrix - dot(up_left, up_right, outer, HIGH)
    down_left = scaled(down_inv, down_sum)
    down_right = scaled(down_inv, down_term) / replicas
    down_error = down_matrix - dot(down_left, down_right, outer, HIGH)
    up_left, up_right, down_left, down_right = up_left.T, up_right.T, down_left.T, down_right.T
    return (input_grad, up_error[None], up_left, up_right, down_error[None], down_left, down_right)


def solution(mesh):
    return jax.shard_map(
        shards,
        mesh=mesh,
        in_specs=(
            P("dp", "tensor"),
            P("dp", "tensor"),
            P("dp", "tensor"),
            P("tensor", "dp"),
            P("dp", None, "tensor"),
            P("dp", "tensor", None),
            P("tensor", None),
            P(),
        ),
        out_specs=(
            P("dp", "tensor"),
            P("dp", None, "tensor"),
            P(),
            P("tensor", None),
            P("dp", "tensor", None),
            P("tensor", None),
            P(),
        ),
        check_vma=False,
    )
```
